32 devices in a mesh: groups: 2 (over y), pb: 4 (over z), pt: 2 (over x), spin: 2 (over core).
Axes of the slice: x: 2, y: 2, z: 4, core: 2. Of those that a mesh axis runs over, the one named last changes fastest.
Arguments:
- amplitudes: float32 [4, 4, 2048], P(('groups', 'spin'), 'pb'), parts along dimension 0, may hold values from -6 to 6
- valence_orbitals: float32 [4, 4, 32, 1024], P(('groups', 'spin'), 'pb', None, 'pt'), parts along dimension 0, may hold values from -1 to 1
- conduction_orbitals: float32 [4, 4, 64, 1024], P(('groups', 'spin'), 'pb', None, 'pt'), parts along dimension 0, may hold values from -0.75 to 0.75
- screened: float32 [8, 1024, 1024], P(('groups', 'pb'), 'pt'), parts along dimension 0, may hold values from -0.125 to 0.125
- band_gaps: float32 [4, 4, 2048], P(('groups', 'spin'), 'pb', 'pt'), parts along dimension 0, may hold values from 0.5 to 2
- shifts: float32 [4], P(('groups', 'spin')), parts along dimension 0, may hold values from 0.2 to 1
- difference_table: int32 [4, 4], replicated, may hold values from 0 to 3, as said below
Outputs:
- corrections: float32 [4, 4, 2048], P(('groups', 'spin'), 'pb', 'pt'), parts along dimension 0
The draws below stay inside these ranges and needn't reach their ends.
There are 2 independent parts, one for each index of `groups`. The reference program is written for one: setup_inputs(seed, part) draws one part's arguments, and reference() takes and returns one part's arrays. A program takes and returns all parts, laid end to end along the dimension named above; an argument that names none is the same for every part. Nothing has to cross between parts.
Inputs may be any that keep to these rules, and one draw needn't show every extreme that they name: Every column of difference_table is a permutation of the 4 k-points: entry [k, q] is the k-point k - q on the k-point grid.
All inputs are finite; a program needn't handle non-finite values.
Results may differ from the reference program's by a relative error of at most 0.0003.
Values sent between devices are 32-bit elements; how exact they have to be, the bound alone decides.
A program may use at most 64 MiB of HBM per device.

```python
import jax
import jax.numpy as jnp
from jax import lax

S = 2
NV = 32
NC = 64
NP = 1024
K = 4


def draw_difference_table(key, part):
    key = jax.random.fold_in(key, 11)
    key_points, key_shift = jax.random.split(key)
    labels = jax.random.permutation(key_points, K).astype(jnp.int32)
    transfers = jax.random.permutation(key_shift, K).astype(jnp.int32)
    inverse = jnp.zeros((K,), jnp.int32).at[labels].set(jnp.arange(K, dtype=jnp.int32))
    grid = (labels[:, None] - transfers[None, :]) % K
    return inverse[grid].astype(jnp.int32)


def shard_levels(stream_key, dims, shards, least, largest):
    gain = 1.0
    for position, shards_of in shards:
        steps = jax.random.uniform(jax.random.fold_in(jax.random.fold_in(stream_key, 6), position), (shards_of,), jnp.float32, least / len(shards), largest / len(shards))
        gain = gain * jnp.repeat(jnp.exp(steps), dims[position] // shards_of).reshape((-1,) + (1,) * (len(dims) - 1 - position))
    return gain


def noise(own_key, extent, spread, reach, cuts=(), kind=jnp.bfloat16):
    gain = shard_levels(own_key, extent, cuts, -0.22, 0.18) if cuts else 1.0
    values = jax.random.normal(own_key, extent, jnp.float32) * spread * gain
    return jnp.minimum(jnp.maximum(values, -reach), reach).astype(kind)


def setup_inputs(seed: int = 0, part: int = 0) -> dict:
    streams_of = jax.random.split(jax.random.key(seed), 8)
    part_keys = jax.random.split(jax.random.fold_in(streams_of[7], part), 8)
    amplitudes = noise(part_keys[0], (S, K, NV * NC), 1.0, 6.0, ((0, 2), (1, 4)), jnp.float32)
    valence_orbitals = noise(part_keys[1], (S, K, NV, NP), NV ** -0.5, 1.0, ((0, 2), (1, 4), (3, 2)), jnp.float32)
    conduction_orbitals = noise(part_keys[2], (S, K, NC, NP), NC ** -0.5, 0.75, ((0, 2), (1, 4), (3, 2)), jnp.float32)
    screened = noise(part_keys[3], (K, NP, NP), (NP * NP * K // (NV * NC)) ** -0.5, 0.125, ((0, 4), (1, 2)), jnp.float32)
    band_gaps = jnp.clip(0.5 + 1.5 * jax.random.uniform(part_keys[4], (S, K, NV * NC), jnp.float32) ** shard_levels(part_keys[4], (S, K, NV * NC), ((0, 2), (1, 4), (2, 2)), -0.2, 0.2), 0.5, 2.0)
    shifts = jnp.clip(0.2 + 0.8 * jax.random.uniform(part_keys[5], (S,), jnp.float32) ** shard_levels(part_keys[5], (S,), ((0, 2),), -0.2, 0.2), 0.2, 1.0)
    difference_table = draw_difference_table(jax.random.fold_in(streams_of[7], 71), part)
    return {"amplitudes": amplitudes, "valence_orbitals": valence_orbitals, "conduction_orbitals": conduction_orbitals, "screened": screened, "band_gaps": band_gaps, "shifts": shifts, "difference_table": difference_table}


def transfer_terms(amplitudes, valence, conduction, weight, sources):
    source_amp = jnp.take(amplitudes, sources, axis=0)
    source_amp = source_amp.reshape(source_amp.shape[0], NV, NC)
    source_val = jnp.take(valence, sources, axis=0)
    source_con = jnp.take(conduction, sources, axis=0)
    mixed = jnp.einsum("kvm,kvc->kcm", source_val, source_amp, precision=lax.Precision.HIGHEST)
    pairs = jnp.einsum("kcm,kcn->kmn", mixed, source_con, precision=lax.Precision.HIGHEST)
    pairs = pairs * weight[None]
    half = jnp.einsum("kvm,kmn->kvn", valence, pairs, precision=lax.Precision.HIGHEST)
    result = jnp.einsum("kvn,kcn->kvc", half, conduction, precision=lax.Precision.HIGHEST)
    return result.reshape(result.shape[0], NV * NC)


def reference(amplitudes, valence_orbitals, conduction_orbitals, screened, band_gaps, shifts, difference_table):
    channels = []
    for channel in range(S):
        def add_transfer(total, inputs):
            column, weight = inputs
            sources = jnp.take(difference_table, column, axis=1).astype(jnp.int32)
            term = transfer_terms(amplitudes[channel], valence_orbitals[channel], conduction_orbitals[channel], weight, sources)
            return total + term, None

        start = jnp.zeros((K, NV * NC), jnp.float32)
        total, unused = lax.scan(add_transfer, start, (jnp.arange(K, dtype=jnp.int32), screened))
        channels.append(total)
    direct = jnp.stack(channels)
    return (band_gaps * amplitudes - direct) / (band_gaps + shifts[:, None, None])
```

```python
import functools

import jax
import jax.numpy as jnp
from jax import lax
from jax.experimental import pallas as pl
from jax.experimental.pallas import tpu as pltpu
from jax.sharding import PartitionSpec as P

F32 = jnp.float32
BF16 = jnp.bfloat16
LANES = 128


def split(x):
    hi = x.astype(BF16)
    return hi, (x - hi.astype(F32)).astype(BF16)


def dot(a, b, dims=((1,), (0,))):
    return lax.dot_general(a, b, (dims, ((), ())), preferred_element_type=F32)


def each(count, body):
    if count <= 4:
        for i in range(count):
            body(i)
    else:
        lax.fori_loop(0, count, lambda i, _: (body(i), 0)[1], 0)


def kernel(
    n, m, ch,
    amp_ref, val_ref, con_ref, scr_ref, gap_ref, shift_ref, table_ref,
    out_ref,
    amp_all, val_all, con_all, weight, gaps,
    amp_wide, val_stack, con_stack, mix, half_stack, part, inbox, total,
    load_sem, amp_send, amp_recv, val_send, val_recv, con_recv,
    conz_send, conx_send, part_send, part_recv,
):
    nv, slab = val_ref.shape
    nc = con_ref.shape[0]
    w = slab // ch
    q = lax.axis_index("pb")
    p = lax.axis_index("pt")

    def at(z, x):
        return {"pb": z, "pt": x}

    def remote(src, dst, send, recv, z, x):
        return pltpu.make_async_remote_copy(
            src_ref=src, dst_ref=dst, send_sem=send, recv_sem=recv,
            device_id=at(z, x), device_id_type=pl.DeviceIdType.MESH,
        )

    barrier = pltpu.get_barrier_semaphore()
    for dz in range(n):
        for dx in range(m):
            if dz or dx:
                pl.semaphore_signal(
                    barrier, inc=1, device_id=at(lax.rem(q + dz, n), lax.rem(p + dx, m)),
                    device_id_type=pl.DeviceIdType.MESH,
                )

    loads = [
        pltpu.make_async_copy(amp_ref, amp_all.at[q], load_sem.at[0]),
        pltpu.make_async_copy(val_ref, val_all.at[q], load_sem.at[1]),
        pltpu.make_async_copy(gap_ref, gaps, load_sem.at[2]),
        pltpu.make_async_copy(scr_ref, weight, load_sem.at[3]),
    ] + [
        pltpu.make_async_copy(
            con_ref.at[:, pl.ds(c * w, w)], con_all.at[q, p, c], load_sem.at[4 + c]
        )
        for c in range(ch)
    ]
    for load in loads:
        load.start()

    pl.semaphore_wait(barrier, n * m - 1)

    def val_copy(z):
        return remote(val_ref, val_all.at[q], val_send.at[z], val_recv.at[q], z, p)

    def amp_copy(z):
        return remote(amp_ref, amp_all.at[q], amp_send.at[z], amp_recv.at[q], z, p)

    def send_small(d):
        z = lax.rem(q + d + 1, n)
        amp_copy(z).start()
        val_copy(z).start()

    each(n - 1, send_small)

    def con_z(s, c, side, src):
        z = q - 1 if side == 0 else q + 1
        return remote(
            src, con_all.at[s, p, c], conz_send.at[s, c, side], con_recv.at[s, p, c], z, p
        )

    def con_x(s, c, dx, src):
        x = lax.rem(p + dx, m)
        return remote(
            src, con_all.at[s, p, c], conx_send.at[s, dx - 1, c], con_recv.at[s, p, c], q, x
        )

    def con_wait(s, x, c):
        block = con_all.at[s, x, c]
        pltpu.make_async_remote_copy(
            src_ref=block, dst_ref=block, send_sem=conz_send.at[s, c, 0],
            recv_sem=con_recv.at[s, x, c], device_id=at(q, lax.rem(p + 1, m)),
            device_id_type=pl.DeviceIdType.MESH,
        ).wait_recv()

    for c in range(ch):
        own = con_ref.at[:, pl.ds(c * w, w)]

        @pl.when(q > 0)
        def _():
            con_z(q, c, 0, own).start()

        @pl.when(q < n - 1)
        def _():
            con_z(q, c, 1, own).start()

        for dx in range(1, m):
            con_x(q, c, dx, own).start()

    def prepare(s):
        rows = amp_all[s]
        turned = pltpu.roll(rows, LANES // 2, 1)
        low = lax.broadcasted_iota(jnp.int32, rows.shape, 1) < LANES // 2
        amp_wide[pl.ds(0, nv // 2, stride=2), :] = jnp.where(low, rows, turned)
        amp_wide[pl.ds(1, nv // 2, stride=2), :] = jnp.where(low, turned, rows)
        a_hi, a_lo = split(amp_wide[pl.ds(0, nv), :])
        v_hi, v_lo = split(val_all[s])
        both = jnp.concatenate([v_hi, v_lo], axis=0)
        val_stack[s] = both
        mixed = dot(
            jnp.concatenate([both, both], axis=0),
            jnp.concatenate([a_hi, a_hi, a_lo, a_lo], axis=0),
            ((0,), (0,)),
        )
        hi = mixed.astype(BF16).astype(F32)
        left = lax.broadcasted_iota(jnp.int32, mixed.shape, 1) < LANES // 2
        pair = jnp.where(left, hi, mixed - hi).astype(BF16)
        mix[s] = jnp.concatenate([pair, pair], axis=1)

    def target_of(s):
        if n <= 8:
            found = jnp.int32(0)
            for k in range(1, n):
                found = jnp.where(table_ref[k, q] == s, k, found)
            return found
        return lax.fori_loop(
            0, n, lambda k, f: jnp.where(table_ref[k, q] == s, k, f), jnp.int32(0)
        )

    def unit(s, x, c, target):
        c_hi, c_lo = split(con_all[s, x, c])
        stack = jnp.concatenate([c_hi, c_hi, c_lo, c_lo], axis=0)
        con_stack[s, x, c] = stack
        columns = pl.ds(pl.multiple_of(x * slab + c * w, w), w)
        pairs = dot(mix[s], stack) * weight[:, columns]
        p_hi, p_lo = split(pairs)
        bands = val_stack[target]
        both = dot(bands, p_hi) + dot(bands, p_lo)
        half = both[:nv] + both[nv:]
        h_hi, h_lo = split(half)
        half_stack[s, x, c] = jnp.concatenate([h_hi, h_lo], axis=0)

    def units(s, x):
        target = target_of(s)
        lax.fori_loop(0, ch, lambda c, _: (unit(s, x, c, target), 0)[1], 0)

    def crossed(s):
        target = target_of(s)

        def step(i, _):
            x = lax.rem(p + 1 + lax.div(i, ch), m)
            c = lax.rem(i, ch)
            con_wait(s, x, c)
            unit(s, x, c, target)
            return 0

        lax.fori_loop(0, (m - 1) * ch, step, 0)

    for load in loads:
        load.wait()
    prepare(q)

    def take_small(d):
        s = lax.rem(q + d + 1, n)
        remote(amp_all.at[s], amp_all.at[s], amp_send.at[s], amp_recv.at[s], s, p).wait_recv()
        remote(val_all.at[s], val_all.at[s], val_send.at[s], val_recv.at[s], s, p).wait_recv()
        prepare(s)

    lax.fori_loop(0, n - 1, lambda d, _: (take_small(d), 0)[1], 0)

    units(q, p)

    def forward(s, side):
        for c in range(ch):
            con_wait(s, p, c)
            block = con_all.at[s, p, c]

            @pl.when((q > 0) if side == 0 else (q < n - 1))
            def _():
                con_z(s, c, side, block).start()

            for dx in range(1, m):
                con_x(s, c, dx, block).start()

    def walk(t, _):
        @pl.when(q + t < n)
        def _():
            forward(q + t, 0)

        @pl.when(q - t >= 0)
        def _():
            forward(q - t, 1)

        @pl.when(q + t < n)
        def _():
            units(q + t, p)

        @pl.when(q - t >= 0)
        def _():
            units(q - t, p)

        @pl.when(q + t - 1 < n)
        def _():
            crossed(q + t - 1)

        @pl.when((q - t + 1 >= 0) & (t > 1))
        def _():
            crossed(q - t + 1)

        return 0

    lax.fori_loop(1, n, walk, 0)

    @pl.when(q + n - 1 < n)
    def _():
        crossed(q + n - 1)

    @pl.when((q - n + 1 >= 0) & (n > 1))
    def _():
        crossed(q - n + 1)

    def part_copy(k, x):
        return remote(
            part.at[k, x], inbox.at[q, p], part_send.at[k, x], part_recv.at[q, p], k, x
        )

    rows = nv // m

    def finish(d):
        k = lax.rem(q + d + 1, n)
        source = table_ref[k, q]
        acc = jnp.zeros((2 * nv, 2 * nc), F32)
        for x in range(m):
            for c in range(ch):
                acc = acc + dot(
                    half_stack[source, x, c], con_stack[k, x, c, nc : 3 * nc], ((1,), (1,))
                )
        acc = acc[:nv] + acc[nv:]
        direct = acc[:, :nc] + acc[:, nc:]
        for x in range(m):
            part[k, x] = direct[x * rows : (x + 1) * rows]
        for x in range(m):
            @pl.when((k != q) | (x != p))
            def _():
                part_copy(k, x).start()

    each(n, finish)

    total[pl.ds(0, rows), :] = part[q, p]

    def gather(i):
        z = lax.rem(q + lax.div(i, m), n)
        x = lax.rem(p + lax.rem(i, m), m)
        box = inbox.at[z, x]
        remote(box, box, part_send.at[z, x], part_recv.at[z, x], z, x).wait_recv()
        total[pl.ds(0, rows), :] += inbox[z, x]

    lax.fori_loop(1, n * m, lambda i, _: (gather(i), 0)[1], 0)

    out_rows = out_ref.shape[0]
    even = total[pl.ds(0, out_rows, stride=2), :]
    odd = total[pl.ds(1, out_rows, stride=2), :]
    summed = jnp.concatenate([even, odd], axis=1)
    own_amp = amp_all[q, pl.ds(p * out_rows, out_rows), :]
    gap = gaps[...]
    out_ref[...] = (gap * own_amp - summed) / (gap + shift_ref[0])

    def sent_small(d):
        z = lax.rem(q + d + 1, n)
        amp_copy(z).wait_send()
        val_copy(z).wait_send()

    each(n - 1, sent_small)

    def sent_con(s, _):
        for c in range(ch):
            block = con_all.at[s, p, c]

            @pl.when((q > 0) & (s >= q))
            def _():
                con_z(s, c, 0, block).wait_send()

            @pl.when((q < n - 1) & (s <= q))
            def _():
                con_z(s, c, 1, block).wait_send()

            for dx in range(1, m):
                con_x(s, c, dx, block).wait_send()
        return 0

    lax.fori_loop(0, n, sent_con, 0)

    def sent_part(i):
        z = lax.rem(q + lax.div(i, m), n)
        x = lax.rem(p + lax.rem(i, m), m)
        part_copy(z, x).wait_send()

    lax.fori_loop(1, n * m, lambda i, _: (sent_part(i), 0)[1], 0)


def shards(
    n, m,
    amplitudes, valence_orbitals, conduction_orbitals, screened, band_gaps, shifts, difference_table,
):
    nv, slab = valence_orbitals.shape[2:]
    nc = conduction_orbitals.shape[2]
    ch = 2 if n * m <= 16 else 1
    w = slab // ch
    points = screened.shape[2]
    amp_rows = amplitudes.shape[2] // LANES
    out_rows = band_gaps.shape[2] // LANES
    dma = pltpu.SemaphoreType.DMA
    flat = pl.pallas_call(
        functools.partial(kernel, n, m, ch),
        out_shape=jax.ShapeDtypeStruct((out_rows, LANES), F32),
        in_specs=[pl.BlockSpec(memory_space=pl.ANY)] * 5
        + [pl.BlockSpec(memory_space=pltpu.SMEM)] * 2,
        out_specs=pl.BlockSpec(memory_space=pltpu.VMEM),
        scratch_shapes=[
            pltpu.VMEM((n, amp_rows, LANES), F32),
            pltpu.VMEM((n, nv, slab), F32),
            pltpu.VMEM((n, m, ch, nc, w), F32),
            pltpu.VMEM((slab, points), F32),
            pltpu.VMEM((out_rows, LANES), F32),
            pltpu.VMEM((nv + 8, LANES), F32),
            pltpu.VMEM((n, 2 * nv, slab), BF16),
            pltpu.VMEM((n, m, ch, 4 * nc, w), BF16),
            pltpu.VMEM((n, slab, 4 * nc), BF16),
            pltpu.VMEM((n, m, ch, 2 * nv, w), BF16),
            pltpu.VMEM((n, m, nv // m, nc), F32),
            pltpu.VMEM((n, m, nv // m, nc), F32),
            pltpu.VMEM((nv // m + 8, nc), F32),
            dma((4 + ch,)),
            dma((n,)),
            dma((n,)),
            dma((n,)),
            dma((n,)),
            dma((n, m, ch)),
            dma((n, ch, 2)),
            dma((n, max(m - 1, 1), ch)),
            dma((n, m)),
            dma((n, m)),
        ],
        compiler_params=pltpu.CompilerParams(
            collective_id=0, has_side_effects=True, vmem_limit_bytes=56 * 1024 * 1024
        ),
        cost_estimate=pl.CostEstimate(
            flops=2 * n * slab * points * (nc + nv), bytes_accessed=4 * slab * points,
            transcendentals=0,
        ),
    )(
        amplitudes.reshape(amp_rows, LANES),
        valence_orbitals.reshape(nv, slab),
        conduction_orbitals.reshape(nc, slab),
        screened.reshape(slab, points),
        band_gaps.reshape(out_rows, LANES),
        shifts,
        difference_table,
    )
    return flat.reshape(band_gaps.shape)


def solution(mesh):
    placed = (
        P(("groups", "spin"), "pb", None),
        P(("groups", "spin"), "pb", None, "pt"),
        P(("groups", "spin"), "pb", None, "pt"),
        P(("groups", "pb"), "pt", None),
        P(("groups", "spin"), "pb", "pt"),
        P(("groups", "spin")),
        P(),
    )
    return jax.shard_map(
        functools.partial(shards, mesh.shape["pb"], mesh.shape["pt"]),
        mesh=mesh,
        in_specs=placed,
        out_specs=P(("groups", "spin"), "pb", "pt"),
        check_vma=False,
    )
```

```python
import functools

import jax
import jax.numpy as jnp
from jax import lax
from jax.experimental import pallas as pl
from jax.experimental.pallas import tpu as pltpu
from jax.sharding import PartitionSpec as P

F32 = jnp.float32
BF16 = jnp.bfloat16
LANES = 128


def split(x):
    hi = x.astype(BF16)
    return hi, (x - hi.astype(F32)).astype(BF16)


def dot(a, b, dims=((1,), (0,))):
    return lax.dot_general(a, b, (dims, ((), ())), preferred_element_type=F32)


def each(count, body):
    if count <= 4:
        for i in range(count):
            body(i)
    else:
        lax.fori_loop(0, count, lambda i, _: (body(i), 0)[1], 0)


def kernel(
    n, m, ch, pieces,
    amp_ref, val_ref, con_ref, scr_ref, gap_ref, shift_ref, table_ref,
    out_ref,
    amp_all, val_all, con_all, weight, gaps,
    amp_wide, val_stack, con_stack, mix, half_stack, part, inbox, total,
    load_sem, amp_send, amp_recv, val_send, val_recv,
    con_send, conx_send, con_recv, part_send, part_recv,
):
    nv, slab = val_ref.shape
    nc = con_ref.shape[0]
    w = slab // ch
    q = lax.axis_index("pb")
    p = lax.axis_index("pt")

    def at(z, x):
        return {"pb": z, "pt": x}

    def remote(src, dst, send, recv, z, x):
        return pltpu.make_async_remote_copy(
            src_ref=src, dst_ref=dst, send_sem=send, recv_sem=recv,
            device_id=at(z, x), device_id_type=pl.DeviceIdType.MESH,
        )

    barrier = pltpu.get_barrier_semaphore()
    for dz in range(n):
        for dx in range(m):
            if dz or dx:
                pl.semaphore_signal(
                    barrier, inc=1, device_id=at(lax.rem(q + dz, n), lax.rem(p + dx, m)),
                    device_id_type=pl.DeviceIdType.MESH,
                )

    loads = [
        pltpu.make_async_copy(amp_ref, amp_all.at[q], load_sem.at[0]),
        pltpu.make_async_copy(val_ref, val_all.at[q], load_sem.at[1]),
        pltpu.make_async_copy(gap_ref, gaps, load_sem.at[2]),
        pltpu.make_async_copy(scr_ref, weight, load_sem.at[3]),
        pltpu.make_async_copy(con_ref, con_all.at[q, p], load_sem.at[4]),
    ]
    for load in loads:
        load.start()

    pl.semaphore_wait(barrier, n * m - 1)

    def small_copies(z):
        return (
            remote(val_ref, val_all.at[q], val_send.at[z], val_recv.at[q], z, p),
            remote(amp_ref, amp_all.at[q], amp_send.at[z], amp_recv.at[q], z, p),
        )

    def small_wait(s):
        for ref, send, recv in ((val_all, val_send, val_recv), (amp_all, amp_send, amp_recv)):
            remote(ref.at[s], ref.at[s], send.at[s], recv.at[s], s, p).wait_recv()

    def rows_of(r):
        return pl.ds(r * (nc // pieces), nc // pieces)

    def con_z(s, r, side, src):
        z = q - 1 if side == 0 else q + 1
        spot = con_all.at[s, p, rows_of(r)]
        return remote(src, spot, con_send.at[s, r, side], con_recv.at[s, p, r], z, p)

    def con_x(s, r, dx, src):
        spot = con_all.at[s, p, rows_of(r)]
        return remote(
            src, spot, conx_send.at[s, dx - 1, r], con_recv.at[s, p, r], q, lax.rem(p + dx, m)
        )

    def con_wait(s, x, r):
        spot = con_all.at[s, x, rows_of(r)]
        remote(
            spot, spot, con_send.at[s, r, 0], con_recv.at[s, x, r], q, lax.rem(p + 1, m)
        ).wait_recv()

    def toward(side):
        return (q > 0) if side == 0 else (q < n - 1)

    def both(t, act):
        pl.when(q + t < n)(lambda: act(q + t, 0))
        pl.when(q - t >= 0)(lambda: act(q - t, 1))

    def forward(t):
        for r in range(pieces):
            def take(s, side):
                con_wait(s, p, r)
                block = con_all.at[s, p, rows_of(r)]
                pl.when(toward(side))(lambda: con_z(s, r, side, block).start())
                for dx in range(1, m):
                    con_x(s, r, dx, block).start()

            both(t, take)

    def send_small(d):
        for copy in small_copies(lax.rem(q + d + 1, n)):
            copy.start()

    for r in range(pieces):
        for side in range(2):
            pl.when(toward(side))(lambda: con_z(q, r, side, con_ref.at[rows_of(r)]).start())
        for dx in range(1, m):
            con_x(q, r, dx, con_ref.at[rows_of(r)]).start()
    each(n - 1, send_small)
    if n > 1:
        forward(1)
    if n > 2:
        forward(2)

    def prepare(s):
        rows = amp_all[s]
        turned = pltpu.roll(rows, LANES // 2, 1)
        low = lax.broadcasted_iota(jnp.int32, rows.shape, 1) < LANES // 2
        amp_wide[pl.ds(0, nv // 2, stride=2), :] = jnp.where(low, rows, turned)
        amp_wide[pl.ds(1, nv // 2, stride=2), :] = jnp.where(low, turned, rows)
        a_hi, a_lo = split(amp_wide[pl.ds(0, nv), :])
        v_hi, v_lo = split(val_all[s])
        both = jnp.concatenate([v_hi, v_lo], axis=0)
        val_stack[s] = both
        mixed = dot(
            jnp.concatenate([both, both], axis=0),
            jnp.concatenate([a_hi, a_hi, a_lo, a_lo], axis=0),
            ((0,), (0,)),
        )
        hi = mixed.astype(BF16).astype(F32)
        left = lax.broadcasted_iota(jnp.int32, mixed.shape, 1) < LANES // 2
        pair = jnp.where(left, hi, mixed - hi).astype(BF16)
        mix[s] = jnp.concatenate([pair, pair], axis=1)

    def target_of(s):
        if n <= 8:
            found = jnp.int32(0)
            for k in range(1, n):
                found = jnp.where(table_ref[k, q] == s, k, found)
            return found
        return lax.fori_loop(
            0, n, lambda k, f: jnp.where(table_ref[k, q] == s, k, f), jnp.int32(0)
        )

    def unit(s, x, c, target):
        lanes = pl.ds(pl.multiple_of(c * w, w), w)
        c_hi, c_lo = split(con_all[s, x, :, lanes])
        stack = jnp.concatenate([c_hi, c_hi, c_lo, c_lo], axis=0)
        con_stack[s, x, c] = stack
        columns = pl.ds(pl.multiple_of(x * slab + c * w, w), w)
        pairs = dot(mix[s], stack) * weight[:, columns]
        p_hi, p_lo = split(pairs)
        bands = val_stack[target]
        products = dot(bands, p_hi) + dot(bands, p_lo)
        half = products[:nv] + products[nv:]
        h_hi, h_lo = split(half)
        half_stack[s, x, c] = jnp.concatenate([h_hi, h_lo], axis=0)

    def units(s, x):
        target = target_of(s)
        lax.fori_loop(0, ch, lambda c, _: (unit(s, x, c, target), 0)[1], 0)

    def crossed(s):
        def step(i, _):
            x = lax.rem(p + 1 + i, m)
            for r in range(pieces):
                con_wait(s, x, r)
            units(s, x)
            return 0

        lax.fori_loop(0, m - 1, step, 0)

    for load in loads:
        load.wait()
    prepare(q)

    def take_small(d):
        s = lax.rem(q + d + 1, n)
        small_wait(s)
        prepare(s)

    lax.fori_loop(0, n - 1, lambda d, _: (take_small(d), 0)[1], 0)

    units(q, p)
    crossed(q)

    def walk(t, _):
        both(t - 1, lambda s, side: units(s, p))
        pl.when(t > 2)(lambda: forward(t))
        both(t - 1, lambda s, side: crossed(s))
        return 0

    lax.fori_loop(2, n, walk, 0)
    if n > 1:
        both(n - 1, lambda s, side: units(s, p))
        both(n - 1, lambda s, side: crossed(s))

    def part_copy(k, x):
        return remote(
            part.at[k, x], inbox.at[q, p], part_send.at[k, x], part_recv.at[q, p], k, x
        )

    rows = nv // m

    def finish(d):
        k = lax.rem(q + d + 1, n)
        source = table_ref[k, q]
        acc = jnp.zeros((2 * nv, 2 * nc), F32)
        for x in range(m):
            for c in range(ch):
                acc = acc + dot(
                    half_stack[source, x, c], con_stack[k, x, c, nc : 3 * nc], ((1,), (1,))
                )
        acc = acc[:nv] + acc[nv:]
        direct = acc[:, :nc] + acc[:, nc:]
        for x in range(m):
            part[k, x] = direct[x * rows : (x + 1) * rows]
        for x in range(m):
            @pl.when((k != q) | (x != p))
            def _():
                part_copy(k, x).start()

    each(n, finish)

    def gather(i, summed):
        z = lax.rem(q + lax.div(i, m), n)
        x = lax.rem(p + lax.rem(i, m), m)
        box = inbox.at[z, x]
        remote(box, box, part_send.at[z, x], part_recv.at[z, x], z, x).wait_recv()
        return summed + inbox[z, x]

    summed = part[q, p]
    if n * m <= 16:
        for i in range(1, n * m):
            summed = gather(i, summed)
    else:
        summed = lax.fori_loop(1, n * m, gather, summed)
    total[pl.ds(0, rows), :] = summed

    out_rows = out_ref.shape[0]
    even = total[pl.ds(0, out_rows, stride=2), :]
    odd = total[pl.ds(1, out_rows, stride=2), :]
    summed = jnp.concatenate([even, odd], axis=1)
    own_amp = amp_all[q, pl.ds(p * out_rows, out_rows), :]
    gap = gaps[...]
    out_ref[...] = (gap * own_amp - summed) / (gap + shift_ref[0])

    def sent_small(d):
        for copy in small_copies(lax.rem(q + d + 1, n)):
            copy.wait_send()

    each(n - 1, sent_small)

    def sent_con(s, _):
        for r in range(pieces):
            block = con_all.at[s, p, rows_of(r)]
            pl.when(toward(0) & (s >= q))(lambda: con_z(s, r, 0, block).wait_send())
            pl.when(toward(1) & (s <= q))(lambda: con_z(s, r, 1, block).wait_send())
            for dx in range(1, m):
                con_x(s, r, dx, block).wait_send()
        return 0

    lax.fori_loop(0, n, sent_con, 0)

    def sent_part(i):
        z = lax.rem(q + lax.div(i, m), n)
        x = lax.rem(p + lax.rem(i, m), m)
        part_copy(z, x).wait_send()

    lax.fori_loop(1, n * m, lambda i, _: (sent_part(i), 0)[1], 0)


def shards(
    n, m,
    amplitudes, valence_orbitals, conduction_orbitals, screened, band_gaps, shifts, difference_table,
):
    nv, slab = valence_orbitals.shape[2:]
    nc = conduction_orbitals.shape[2]
    ch = 1
    pieces = 2 if n * m <= 16 else 1
    w = slab // ch
    points = screened.shape[2]
    amp_rows = amplitudes.shape[2] // LANES
    out_rows = band_gaps.shape[2] // LANES
    dma = pltpu.SemaphoreType.DMA
    flat = pl.pallas_call(
        functools.partial(kernel, n, m, ch, pieces),
        out_shape=jax.ShapeDtypeStruct((out_rows, LANES), F32),
        in_specs=[pl.BlockSpec(memory_space=pl.ANY)] * 5
        + [pl.BlockSpec(memory_space=pltpu.SMEM)] * 2,
        out_specs=pl.BlockSpec(memory_space=pltpu.VMEM),
        scratch_shapes=[
            pltpu.VMEM((n, amp_rows, LANES), F32),
            pltpu.VMEM((n, nv, slab), F32),
            pltpu.VMEM((n, m, nc, slab), F32),
            pltpu.VMEM((slab, points), F32),
            pltpu.VMEM((out_rows, LANES), F32),
            pltpu.VMEM((nv + 8, LANES), F32),
            pltpu.VMEM((n, 2 * nv, slab), BF16),
            pltpu.VMEM((n, m, ch, 4 * nc, w), BF16),
            pltpu.VMEM((n, slab, 4 * nc), BF16),
            pltpu.VMEM((n, m, ch, 2 * nv, w), BF16),
            pltpu.VMEM((n, m, nv // m, nc), F32),
            pltpu.VMEM((n, m, nv // m, nc), F32),
            pltpu.VMEM((nv // m + 8, nc), F32),
            dma((5,)),
            dma((n,)),
            dma((n,)),
            dma((n,)),
            dma((n,)),
            dma((n, pieces, 2)),
            dma((n, max(m - 1, 1), pieces)),
            dma((n, m, pieces)),
            dma((n, m)),
            dma((n, m)),
        ],
        compiler_params=pltpu.CompilerParams(
            collective_id=0, has_side_effects=True, vmem_limit_bytes=56 * 1024 * 1024
        ),
        cost_estimate=pl.CostEstimate(
            flops=2 * n * slab * points * (nc + nv), bytes_accessed=4 * slab * points,
            transcendentals=0,
        ),
    )(
        amplitudes.reshape(amp_rows, LANES),
        valence_orbitals.reshape(nv, slab),
        conduction_orbitals.reshape(nc, slab),
        screened.reshape(slab, points),
        band_gaps.reshape(out_rows, LANES),
        shifts,
        difference_table,
    )
    return flat.reshape(band_gaps.shape)


def solution(mesh):
    placed = (
        P(("groups", "spin"), "pb", None),
        P(("groups", "spin"), "pb", None, "pt"),
        P(("groups", "spin"), "pb", None, "pt"),
        P(("groups", "pb"), "pt", None),
        P(("groups", "spin"), "pb", "pt"),
        P(("groups", "spin")),
        P(),
    )
    return jax.shard_map(
        functools.partial(shards, mesh.shape["pb"], mesh.shape["pt"]),
        mesh=mesh,
        in_specs=placed,
        out_specs=P(("groups", "spin"), "pb", "pt"),
        check_vma=False,
    )
```

```python
import functools

import jax
import jax.numpy as jnp
from jax import lax
from jax.experimental import pallas as pl
from jax.experimental.pallas import tpu as pltpu
from jax.sharding import PartitionSpec as P

F32 = jnp.float32
BF16 = jnp.bfloat16
LANES = 128


def split(x):
    hi = x.astype(BF16)
    return hi, (x - hi.astype(F32)).astype(BF16)


def dot(a, b, dims=((1,), (0,))):
    return lax.dot_general(a, b, (dims, ((), ())), preferred_element_type=F32)


def each(count, body):
    if count <= 4:
        for i in range(count):
            body(i)
    else:
        lax.fori_loop(0, count, lambda i, _: (body(i), 0)[1], 0)


def kernel(
    n, m, ch, pieces,
    amp_ref, val_ref, con_ref, scr_ref, gap_ref, shift_ref, table_ref,
    out_ref,
    amp_all, val_all, con_all, weight, gaps,
    amp_wide, val_stack, con_stack, mix, half_stack, part, inbox, total,
    load_sem, amp_send, amp_recv, val_send, val_recv,
    con_send, conx_send, con_recv, part_send, part_recv,
):
    nv, slab = val_ref.shape
    nc = con_ref.shape[0]
    w = slab // ch
    q = lax.axis_index("pb")
    p = lax.axis_index("pt")

    def at(z, x):
        return {"pb": z, "pt": x}

    def remote(src, dst, send, recv, z, x):
        return pltpu.make_async_remote_copy(
            src_ref=src, dst_ref=dst, send_sem=send, recv_sem=recv,
            device_id=at(z, x), device_id_type=pl.DeviceIdType.MESH,
        )

    barrier = pltpu.get_barrier_semaphore()
    for dz in range(n):
        for dx in range(m):
            if dz or dx:
                pl.semaphore_signal(
                    barrier, inc=1, device_id=at(lax.rem(q + dz, n), lax.rem(p + dx, m)),
                    device_id_type=pl.DeviceIdType.MESH,
                )

    loads = [
        pltpu.make_async_copy(amp_ref, amp_all.at[q], load_sem.at[0]),
        pltpu.make_async_copy(val_ref, val_all.at[q], load_sem.at[1]),
        pltpu.make_async_copy(gap_ref, gaps, load_sem.at[2]),
        pltpu.make_async_copy(scr_ref, weight, load_sem.at[3]),
        pltpu.make_async_copy(con_ref, con_all.at[q, p], load_sem.at[4]),
    ]
    for load in loads:
        load.start()

    pl.semaphore_wait(barrier, n * m - 1)

    def small_copies(z):
        return (
            remote(val_ref, val_all.at[q], val_send.at[z], val_recv.at[q], z, p),
            remote(amp_ref, amp_all.at[q], amp_send.at[z], amp_recv.at[q], z, p),
        )

    def small_wait(s):
        for ref, send, recv in ((val_all, val_send, val_recv), (amp_all, amp_send, amp_recv)):
            remote(ref.at[s], ref.at[s], send.at[s], recv.at[s], s, p).wait_recv()

    def rows_of(r):
        return pl.ds(r * (nc // pieces), nc // pieces)

    def con_z(s, r, side, src):
        z = q - 1 if side == 0 else q + 1
        spot = con_all.at[s, p, rows_of(r)]
        return remote(src, spot, con_send.at[s, r, side], con_recv.at[s, p, r], z, p)

    def con_x(s, r, dx, src):
        spot = con_all.at[s, p, rows_of(r)]
        return remote(
            src, spot, conx_send.at[s, dx - 1, r], con_recv.at[s, p, r], q, lax.rem(p + dx, m)
        )

    def con_wait(s, x, r):
        spot = con_all.at[s, x, rows_of(r)]
        remote(
            spot, spot, con_send.at[s, r, 0], con_recv.at[s, x, r], q, lax.rem(p + 1, m)
        ).wait_recv()

    def toward(side):
        return (q > 0) if side == 0 else (q < n - 1)

    def both(t, act):
        pl.when(q + t < n)(lambda: act(q + t, 0))
        pl.when(q - t >= 0)(lambda: act(q - t, 1))

    def forward(t):
        for r in range(pieces):
            def take(s, side):
                con_wait(s, p, r)
                block = con_all.at[s, p, rows_of(r)]
                pl.when(toward(side))(lambda: con_z(s, r, side, block).start())
                for dx in range(1, m):
                    con_x(s, r, dx, block).start()

            both(t, take)

    def send_small(d):
        for copy in small_copies(lax.rem(q + lax.rem(d + n // 2, n - 1) + 1, n)):
            copy.start()

    for r in range(pieces):
        for side in range(2):
            pl.when(toward(side))(lambda: con_z(q, r, side, con_ref.at[rows_of(r)]).start())
        for dx in range(1, m):
            con_x(q, r, dx, con_ref.at[rows_of(r)]).start()
    each(n - 1, send_small)
    if n > 1:
        forward(1)
    if n > 2:
        forward(2)

    def prepare(s):
        rows = amp_all[s]
        turned = pltpu.roll(rows, LANES // 2, 1)
        low = lax.broadcasted_iota(jnp.int32, rows.shape, 1) < LANES // 2
        amp_wide[pl.ds(0, nv // 2, stride=2), :] = jnp.where(low, rows, turned)
        amp_wide[pl.ds(1, nv // 2, stride=2), :] = jnp.where(low, turned, rows)
        a_hi, a_lo = split(amp_wide[pl.ds(0, nv), :])
        v_hi, v_lo = split(val_all[s])
        both = jnp.concatenate([v_hi, v_lo], axis=0)
        val_stack[s] = both
        mixed = dot(
            jnp.concatenate([both, both], axis=0),
            jnp.concatenate([a_hi, a_hi, a_lo, a_lo], axis=0),
            ((0,), (0,)),
        )
        hi = mixed.astype(BF16).astype(F32)
        left = lax.broadcasted_iota(jnp.int32, mixed.shape, 1) < LANES // 2
        pair = jnp.where(left, hi, mixed - hi).astype(BF16)
        mix[s] = jnp.concatenate([pair, pair], axis=1)

    def target_of(s):
        if n <= 8:
            found = jnp.int32(0)
            for k in range(1, n):
                found = jnp.where(table_ref[k, q] == s, k, found)
            return found
        return lax.fori_loop(
            0, n, lambda k, f: jnp.where(table_ref[k, q] == s, k, f), jnp.int32(0)
        )

    def unit(s, x, c, target):
        lanes = pl.ds(pl.multiple_of(c * w, w), w)
        c_hi, c_lo = split(con_all[s, x, :, lanes])
        stack = jnp.concatenate([c_hi, c_hi, c_lo, c_lo], axis=0)
        con_stack[s, x, c] = stack
        columns = pl.ds(pl.multiple_of(x * slab + c * w, w), w)
        pairs = dot(mix[s], stack) * weight[:, columns]
        p_hi, p_lo = split(pairs)
        bands = val_stack[target]
        products = dot(bands, p_hi) + dot(bands, p_lo)
        half = products[:nv] + products[nv:]
        h_hi, h_lo = split(half)
        half_stack[s, x, c] = jnp.concatenate([h_hi, h_lo], axis=0)

    def units(s, x):
        target = target_of(s)
        lax.fori_loop(0, ch, lambda c, _: (unit(s, x, c, target), 0)[1], 0)

    def crossed(s):
        def step(i, _):
            x = lax.rem(p + 1 + i, m)
            for r in range(pieces):
                con_wait(s, x, r)
            units(s, x)
            return 0

        lax.fori_loop(0, m - 1, step, 0)

    for load in loads:
        load.wait()
    prepare(q)

    def take_small(d):
        s = lax.rem(q + d + 1, n)
        small_wait(s)
        prepare(s)

    lax.fori_loop(0, n - 1, lambda d, _: (take_small(d), 0)[1], 0)

    units(q, p)
    crossed(q)

    def walk(t, _):
        both(t - 1, lambda s, side: units(s, p))
        pl.when(t > 2)(lambda: forward(t))
        both(t - 1, lambda s, side: crossed(s))
        return 0

    lax.fori_loop(2, n, walk, 0)
    if n > 1:
        both(n - 1, lambda s, side: units(s, p))
        both(n - 1, lambda s, side: crossed(s))

    def part_copy(k, x):
        return remote(
            part.at[k, x], inbox.at[q, p], part_send.at[k, x], part_recv.at[q, p], k, x
        )

    rows = nv // m

    def finish(d):
        k = lax.rem(q + d + 1, n)
        source = table_ref[k, q]
        acc = jnp.zeros((2 * nv, 2 * nc), F32)
        for x in range(m):
            for c in range(ch):
                acc = acc + dot(
                    half_stack[source, x, c], con_stack[k, x, c, nc : 3 * nc], ((1,), (1,))
                )
        acc = acc[:nv] + acc[nv:]
        direct = acc[:, :nc] + acc[:, nc:]
        for x in range(m):
            part[k, x] = direct[x * rows : (x + 1) * rows]
        for x in range(m):
            @pl.when((k != q) | (x != p))
            def _():
                part_copy(k, x).start()

    each(n, finish)

    def gather(i, summed):
        z = lax.rem(q + lax.div(i, m), n)
        x = lax.rem(p + lax.rem(i, m), m)
        box = inbox.at[z, x]
        remote(box, box, part_send.at[z, x], part_recv.at[z, x], z, x).wait_recv()
        return summed + inbox[z, x]

    summed = part[q, p]
    if n * m <= 16:
        for i in range(1, n * m):
            summed = gather(i, summed)
    else:
        summed = lax.fori_loop(1, n * m, gather, summed)
    total[pl.ds(0, rows), :] = summed

    out_rows = out_ref.shape[0]
    even = total[pl.ds(0, out_rows, stride=2), :]
    odd = total[pl.ds(1, out_rows, stride=2), :]
    summed = jnp.concatenate([even, odd], axis=1)
    own_amp = amp_all[q, pl.ds(p * out_rows, out_rows), :]
    gap = gaps[...]
    out_ref[...] = (gap * own_amp - summed) / (gap + shift_ref[0])

    def sent_small(d):
        for copy in small_copies(lax.rem(q + d + 1, n)):
            copy.wait_send()

    each(n - 1, sent_small)

    def sent_con(s, _):
        for r in range(pieces):
            block = con_all.at[s, p, rows_of(r)]
            pl.when(toward(0) & (s >= q))(lambda: con_z(s, r, 0, block).wait_send())
            pl.when(toward(1) & (s <= q))(lambda: con_z(s, r, 1, block).wait_send())
            for dx in range(1, m):
                con_x(s, r, dx, block).wait_send()
        return 0

    lax.fori_loop(0, n, sent_con, 0)

    def sent_part(i):
        z = lax.rem(q + lax.div(i, m), n)
        x = lax.rem(p + lax.rem(i, m), m)
        part_copy(z, x).wait_send()

    lax.fori_loop(1, n * m, lambda i, _: (sent_part(i), 0)[1], 0)


def shards(
    n, m,
    amplitudes, valence_orbitals, conduction_orbitals, screened, band_gaps, shifts, difference_table,
):
    nv, slab = valence_orbitals.shape[2:]
    nc = conduction_orbitals.shape[2]
    ch = 1
    pieces = 2 if n * m <= 16 else 1
    w = slab // ch
    points = screened.shape[2]
    amp_rows = amplitudes.shape[2] // LANES
    out_rows = band_gaps.shape[2] // LANES
    dma = pltpu.SemaphoreType.DMA
    flat = pl.pallas_call(
        functools.partial(kernel, n, m, ch, pieces),
        out_shape=jax.ShapeDtypeStruct((out_rows, LANES), F32),
        in_specs=[pl.BlockSpec(memory_space=pl.ANY)] * 5
        + [pl.BlockSpec(memory_space=pltpu.SMEM)] * 2,
        out_specs=pl.BlockSpec(memory_space=pltpu.VMEM),
        scratch_shapes=[
            pltpu.VMEM((n, amp_rows, LANES), F32),
            pltpu.VMEM((n, nv, slab), F32),
            pltpu.VMEM((n, m, nc, slab), F32),
            pltpu.VMEM((slab, points), F32),
            pltpu.VMEM((out_rows, LANES), F32),
            pltpu.VMEM((nv + 8, LANES), F32),
            pltpu.VMEM((n, 2 * nv, slab), BF16),
            pltpu.VMEM((n, m, ch, 4 * nc, w), BF16),
            pltpu.VMEM((n, slab, 4 * nc), BF16),
            pltpu.VMEM((n, m, ch, 2 * nv, w), BF16),
            pltpu.VMEM((n, m, nv // m, nc), F32),
            pltpu.VMEM((n, m, nv // m, nc), F32),
            pltpu.VMEM((nv // m + 8, nc), F32),
            dma((5,)),
            dma((n,)),
            dma((n,)),
            dma((n,)),
            dma((n,)),
            dma((n, pieces, 2)),
            dma((n, max(m - 1, 1), pieces)),
            dma((n, m, pieces)),
            dma((n, m)),
            dma((n, m)),
        ],
        compiler_params=pltpu.CompilerParams(
            collective_id=0, has_side_effects=True, vmem_limit_bytes=56 * 1024 * 1024
        ),
        cost_estimate=pl.CostEstimate(
            flops=2 * n * slab * points * (nc + nv), bytes_accessed=4 * slab * points,
            transcendentals=0,
        ),
    )(
        amplitudes.reshape(amp_rows, LANES),
        valence_orbitals.reshape(nv, slab),
        conduction_orbitals.reshape(nc, slab),
        screened.reshape(slab, points),
        band_gaps.reshape(out_rows, LANES),
        shifts,
        difference_table,
    )
    return flat.reshape(band_gaps.shape)


def solution(mesh):
    placed = (
        P(("groups", "spin"), "pb", None),
        P(("groups", "spin"), "pb", None, "pt"),
        P(("groups", "spin"), "pb", None, "pt"),
        P(("groups", "pb"), "pt", None),
        P(("groups", "spin"), "pb", "pt"),
        P(("groups", "spin")),
        P(),
    )
    return jax.shard_map(
        functools.partial(shards, mesh.shape["pb"], mesh.shape["pt"]),
        mesh=mesh,
        in_specs=placed,
        out_specs=P(("groups", "spin"), "pb", "pt"),
        check_vma=False,
    )
```
